768 devices in a mesh: inner: 48 (over y, z_lo), outer: 16 (over x, z_hi, core).
Axes of the slice: x: 4, y: 8, z: 12 (z_hi: 2, z_lo: 6; z = z_hi * 6 + z_lo), core: 2. Of those that a mesh axis runs over, the one named last changes fastest.
Arguments:
- mentor_picture_vectors: bfloat16 [196608, 1152], P(('inner', 'outer')), may hold values from -1 to 1
- learner_picture_vectors: bfloat16 [196608, 768], P(('inner', 'outer')), may hold values from -1 to 1
- mentor_caption_vectors: bfloat16 [196608, 1152], P(('inner', 'outer')), may hold values from -1 to 1
- learner_caption_vectors: bfloat16 [196608, 768], P(('inner', 'outer')), may hold values from -1 to 1
- matching_round_lookup: int32 [196608], P(('inner', 'outer')), may hold values from 0 to 4
- sharpness_factor: float32 [], replicated, may hold values from 2 to 8
- learned_offset: float32 [], replicated, may hold values from -3 to -1
Outputs:
- image_grad: float32 [196608, 768], P(('inner', 'outer'))
- text_grad: float32 [196608, 768], P(('inner', 'outer'))
The draws below stay inside these ranges and needn't reach their ends.
All inputs are finite; a program needn't handle non-finite values.
Results may differ from the reference program's by a relative error of at most 0.0018.
Values may be sent and summed in bfloat16 or wider, within the bound.
A program may use at most 32 MiB of HBM per device.

```python
import math
import jax
import jax.numpy as jnp
from jax import lax

DT = 1152
DS = 768
TOK_DEV = 256
INNER_STEPS = 4
CAPTION_SLAB_NUM = 5
TOKENS = 196608
N_INNER = 48
N_OUTER = 16


def touch_ends(array, key, least, top_value):
    longest = array.shape.index(max(array.shape))
    spots = []
    for shift in (0, 1):
        where = [jax.random.randint(jax.random.fold_in(key, axis), (), 0, length) for axis, length in enumerate(array.shape)]
        where[longest] = (where[longest] + shift) % array.shape[longest]
        spots.append(tuple(where))
    return array.at[spots[0]].set(least).at[spots[1]].set(top_value)


def shard_levels(key, dims, pieces, least, top_value):
    loudness = 1.0
    for position, shards_of in pieces:
        draws = jax.random.uniform(jax.random.fold_in(jax.random.fold_in(key, 6), position), (shards_of,), jnp.float32, least / len(pieces), top_value / len(pieces))
        loudness = loudness * jnp.repeat(jnp.exp(draws), dims[position] // shards_of).reshape((-1,) + (1,) * (len(dims) - 1 - position))
    return loudness


def normal_values(own_key, extent, deviation, reach, shards=(), kind=jnp.bfloat16):
    array = deviation * jax.random.normal(own_key, extent, jnp.float32)
    if shards:
        array = array * shard_levels(own_key, extent, shards, -0.22, 0.18)
    return jnp.clip(array, -reach, reach).astype(kind)


def setup_inputs(seed: int = 0) -> dict:
    keys = jax.random.split(jax.random.key(seed), 8)
    mentor_picture_vectors = normal_values(keys[0], (TOKENS, DT), (1.0 / DT ** 0.25), 1.0, ((0, 768),))
    learner_picture_vectors = normal_values(keys[1], (TOKENS, DS), (1.0 / DS ** 0.25), 1.0, ((0, 768),))
    mentor_caption_vectors = normal_values(keys[2], (TOKENS, DT), (1.0 / DT ** 0.25), 1.0, ((0, 768),))
    learner_caption_vectors = normal_values(keys[3], (TOKENS, DS), (1.0 / DS ** 0.25), 1.0, ((0, 768),))
    matching_round_lookup = touch_ends(jax.random.randint(keys[4], (TOKENS,), 0, CAPTION_SLAB_NUM), jax.random.fold_in(keys[4], 1), 0, CAPTION_SLAB_NUM - 1).astype(jnp.int32)
    sharpness_factor = jnp.clip(jnp.exp(jax.random.uniform(keys[5], (), jnp.float32, math.log(2.0), math.log(8.0))), 2.0, 8.0)
    learned_offset = jnp.clip(jax.random.uniform(keys[6], (), jnp.float32, -3.0, -1.0), -3.0, -1.0)
    return {"mentor_picture_vectors": mentor_picture_vectors, "learner_picture_vectors": learner_picture_vectors, "mentor_caption_vectors": mentor_caption_vectors, "learner_caption_vectors": learner_caption_vectors, "matching_round_lookup": matching_round_lookup, "sharpness_factor": sharpness_factor, "learned_offset": learned_offset}


def round_loss_pieces(mentor_picture_embedding, learner_picture_embedding, mentor_caption_embedding, learner_caption_embedding, desired_signs, round_tally, sharpness_factor, learned_offset):
    teacher = jnp.einsum("syc,smc->sym", mentor_picture_embedding.astype(jnp.float32), mentor_caption_embedding.astype(jnp.float32))
    prob = jax.nn.sigmoid(4.0 * teacher - 2.0)
    learner_network = sharpness_factor * jnp.einsum("syc,smc->sym", learner_picture_embedding.astype(jnp.float32), learner_caption_embedding.astype(jnp.float32)) + learned_offset
    rows = TOK_DEV
    diag = jnp.eye(rows, dtype=jnp.float32)
    hits = (desired_signs == round_tally).astype(jnp.float32)
    target = 0.5 * (hits[:, :, None] * diag[None] + prob)
    grad = (jax.nn.sigmoid(learner_network) - target).astype(jnp.bfloat16)
    picture_shard = jnp.einsum("obc,ocd->obd", grad.astype(jnp.float32), learner_caption_embedding.astype(jnp.float32))
    caption_shard = jnp.einsum("obc,obd->ocd", grad.astype(jnp.float32), learner_picture_embedding.astype(jnp.float32))
    return picture_shard, caption_shard


def reference(mentor_picture_vectors, learner_picture_vectors, mentor_caption_vectors, learner_caption_vectors, matching_round_lookup, sharpness_factor, learned_offset):
    shape_t = (N_INNER, N_OUTER, TOK_DEV, DT)
    shape_s = (N_INNER, N_OUTER, TOK_DEV, DS)
    mentor_picture_embedding = mentor_picture_vectors.reshape(shape_t)
    learner_picture_embedding = learner_picture_vectors.reshape(shape_s)
    mentor_caption_embedding = mentor_caption_vectors.reshape(shape_t)
    learner_caption_embedding = learner_caption_vectors.reshape(shape_s)
    desired_signs = matching_round_lookup.reshape(N_INNER, N_OUTER, TOK_DEV)
    outer_ids = jnp.arange(N_OUTER, dtype=jnp.int32)

    def per_inner(slab_ordinal):
        img_grad = jnp.zeros((N_OUTER, TOK_DEV, DS), jnp.float32)
        parts = []
        for round_tally in range(CAPTION_SLAB_NUM):
            if round_tally < INNER_STEPS:
                src_i = (slab_ordinal - round_tally) % N_INNER
                src_o = outer_ids
            else:
                src_i = (slab_ordinal - INNER_STEPS + 1) % N_INNER
                src_o = (outer_ids - 1) % N_OUTER
            mentor_shard = mentor_caption_embedding[src_i][src_o]
            learner_shard = learner_caption_embedding[src_i][src_o]
            picture_shard, caption_shard = round_loss_pieces(mentor_picture_embedding[slab_ordinal], learner_picture_embedding[slab_ordinal], mentor_shard, learner_shard, desired_signs[slab_ordinal], round_tally, sharpness_factor, learned_offset)
            img_grad = img_grad + picture_shard
            parts.append(caption_shard)
        return img_grad, jnp.stack(parts)

    img_grad, txt_parts = lax.map(per_inner, jnp.arange(N_INNER, dtype=jnp.int32))
    affinity_multiplier = sharpness_factor / CAPTION_SLAB_NUM
    total = txt_parts[:, INNER_STEPS]
    for round_tally in range(INNER_STEPS):
        moved = jnp.roll(jnp.roll(txt_parts[:, round_tally], INNER_STEPS - 1 - round_tally, axis=0), 1, axis=1)
        total = total + moved
    image_grad = (affinity_multiplier * img_grad).reshape(TOKENS, DS)
    text_grad = (affinity_multiplier * total).reshape(TOKENS, DS)
    return image_grad, text_grad
```

```python
import jax
import jax.numpy as jnp
from jax import lax
from jax.experimental import pallas as pl
from jax.experimental.pallas import tpu as pltpu
from jax.sharding import PartitionSpec as P

STEPS = 5
WIRE = jnp.int16
TOP = 32000.0
MESH = pl.DeviceIdType.MESH


def kernel(n_inner, n_outer, scalars, mi, li, mt, lt, look, img_out, txt_out,
           tm, tl, im, il, lk, acc_img, acc_txt, gsend, grecv, msend, mrecv,
           lsem, tm_s, tl_s, tm_r, tl_r, i_s, i_r, g_s, g_r, m_s, m_r):
    i, o = lax.axis_index("inner"), lax.axis_index("outer")
    c = lax.rem(o, 2)
    at = lambda d: lax.rem(i + d + n_inner, n_inner)
    up, down = lax.rem(o + 1, n_outer), lax.rem(o + n_outer - 1, n_outer)
    rows = tm.shape[1]

    def copy(src, dst, ss, rs, dev):
        return pltpu.make_async_remote_copy(
            src_ref=src, dst_ref=dst, send_sem=ss, recv_sem=rs, device_id=dev, device_id_type=MESH)

    def signal(dev):
        pl.semaphore_signal(barrier, inc=1, device_id=dev, device_id_type=MESH)

    local = [
        pltpu.make_async_copy(mi, im.at[0], lsem.at[0]),
        pltpu.make_async_copy(li, il.at[0], lsem.at[1]),
        pltpu.make_async_copy(mt, tm.at[0], lsem.at[2]),
        pltpu.make_async_copy(lt, tl.at[0], lsem.at[3]),
        pltpu.make_async_copy(look, lk.at[0], lsem.at[4]),
    ]
    def text_next(k, dev):
        return (copy(tm.at[k], tm.at[k + 1], tm_s.at[k], tm_r.at[k + 1], dev),
                copy(tl.at[k], tl.at[k + 1], tl_s.at[k], tl_r.at[k + 1], dev))

    def text_last(k, dev):
        return (copy(tm.at[k], tm.at[4], tm_s.at[3], tm_r.at[4], dev),
                copy(tl.at[k], tl.at[4], tl_s.at[3], tl_r.at[4], dev))

    def image_back():
        dev = (at(-2), o)
        return (copy(im.at[0], im.at[1], i_s.at[0], i_r.at[0], dev),
                copy(il.at[0], il.at[1], i_s.at[1], i_r.at[1], dev),
                copy(lk.at[0], lk.at[1], i_s.at[2], i_r.at[2], dev))

    def grad(k, slot, dev):
        return (copy(msend.at[k], mrecv.at[slot], m_s.at[k], m_r.at[slot], dev),
                copy(gsend.at[k], grecv.at[slot], g_s.at[k], g_r.at[slot], dev))

    def send_grad(k, slot, dev, x):
        top = jnp.maximum(jnp.max(jnp.abs(x)), 1e-30)
        msend[k] = jnp.full(msend.shape[1:], top, jnp.float32)
        gsend[k] = jnp.round(x * (TOP / top)).astype(jnp.int32).astype(WIRE)
        for cp in grad(k, slot, dev):
            cp.start()

    def received(slot):
        for cp in grad(0, slot, (i, o)):
            cp.wait_recv()
        return grecv[slot].astype(jnp.int32).astype(jnp.float32) * (mrecv[slot, 0:1, 0:1] * (1.0 / TOP))

    for cp in local:
        cp.start()
    barrier = pltpu.get_barrier_semaphore()
    signal((at(-1), o))

    @pl.when(c == 0)
    def _():
        signal((at(-3), down))
        pl.semaphore_wait(barrier, 2)

    @pl.when(c == 1)
    def _():
        signal((at(2), o))
        signal((at(1), o))
        signal((at(-2), o))
        signal((i, down))
        pl.semaphore_wait(barrier, 5)

    for cp in local:
        cp.wait()
    for cp in text_next(0, (at(1), o)):
        cp.start()

    @pl.when(c == 1)
    def _():
        for cp in image_back():
            cp.start()
        for cp in text_last(0, (at(3), up)):
            cp.start()

    acc_img[...] = jnp.zeros_like(acc_img)
    acc_txt[...] = jnp.zeros_like(acc_txt)
    sharp, offset = scalars[0], scalars[1]

    def step(s, carry):
        u = lax.rem(s // 2, 2)
        a, b = c * u, s - 2 * c * u

        @pl.when((c == 0) & (s > 0) & (s < 3))
        def _():
            for w, cp in zip(text_next(s - 1, (i, o)), text_next(s, (at(1), o))):
                w.wait_recv()
                cp.start()

        @pl.when((c == 0) & (s == 3))
        def _():
            for w, cp in zip(text_next(2, (i, o)), text_last(3, (i, up))):
                w.wait_recv()
                cp.start()

        @pl.when((c == 1) & (s == 1))
        def _():
            for w in text_next(0, (i, o)):
                w.wait_recv()

        @pl.when((c == 1) & (s == 2))
        def _():
            for w in image_back():
                w.wait_recv()

        @pl.when(s == 4)
        def _():
            for w in text_last(0, (i, o)):
                w.wait_recv()

        dims = (((1,), (1,)), ((), ()))
        teacher = lax.dot_general(im[a], tm[b], dims, preferred_element_type=jnp.float32)
        prob = jax.nn.sigmoid(4.0 * teacher - 2.0)
        student = sharp * lax.dot_general(
            il[a], tl[b], dims, preferred_element_type=jnp.float32) + offset
        r = lax.broadcasted_iota(jnp.int32, (rows, rows), 0)
        q = lax.broadcasted_iota(jnp.int32, (rows, rows), 1)
        hit = (r == q) & (lk[a, 0:1, :] == s)
        target = 0.5 * (jnp.where(hit, 1.0, 0.0) + prob)
        g = (jax.nn.sigmoid(student) - target).astype(jnp.bfloat16)
        acc_img[a] += jnp.dot(g, tl[b], preferred_element_type=jnp.float32)
        acc_txt[b] += lax.dot_general(
            g, il[a], (((0,), (0,)), ((), ())), preferred_element_type=jnp.float32)

        @pl.when((c == 0) & (s == 0))
        def _():
            send_grad(0, 1, (at(1), o), acc_txt[0])

        @pl.when((c == 0) & (s > 0) & (s < 3))
        def _():
            send_grad(s, s + 1, (at(1), o), acc_txt[s] + received(s))

        @pl.when((c == 0) & (s == 3))
        def _():
            send_grad(3, 4, (i, up), acc_txt[3] + received(3))

        @pl.when((c == 1) & (s == 3))
        def _():
            send_grad(1, 1, (at(-1), o), acc_txt[1])
            send_grad(4, 0, (at(2), o), acc_img[1])
            send_grad(0, 4, (at(3), up), acc_txt[0] + received(1))

        return carry

    lax.fori_loop(0, STEPS, step, 0)
    scale = sharp / STEPS

    @pl.when(c == 0)
    def _():
        img_out[...] = scale * acc_img[0]

    @pl.when(c == 1)
    def _():
        img_out[...] = scale * (acc_img[0] + received(0))

    txt_out[...] = scale * (acc_txt[4] + received(4))

    def sent(copies):
        for cp in copies:
            cp.wait_send()

    sent(text_next(0, (i, o)) + text_last(0, (i, o)))
    sent(grad(0, 4, (i, o)) + grad(1, 4, (i, o)))

    @pl.when(c == 0)
    def _():
        sent(text_next(1, (i, o)) + text_next(2, (i, o)))
        sent(grad(2, 4, (i, o)) + grad(3, 4, (i, o)))

    @pl.when(c == 1)
    def _():
        sent(image_back() + grad(4, 0, (i, o)))


def solution(mesh):
    n_inner, n_outer = mesh.shape["inner"], mesh.shape["outer"]

    def shards(mi, li, mt, lt, lookup, sharpness, offset):
        rows, dt = mi.shape
        ds = li.shape[1]
        scalars = jnp.stack([sharpness, offset])
        look = jnp.broadcast_to(lookup[None, :], (8, rows))
        hbm = pl.BlockSpec(memory_space=pl.ANY)
        vmem = pl.BlockSpec(memory_space=pltpu.VMEM)
        bf, f32, dma = jnp.bfloat16, jnp.float32, pltpu.SemaphoreType.DMA
        return pl.pallas_call(
            lambda *refs: kernel(n_inner, n_outer, *refs),
            out_shape=(jax.ShapeDtypeStruct((rows, ds), f32), jax.ShapeDtypeStruct((rows, ds), f32)),
            in_specs=[pl.BlockSpec(memory_space=pltpu.SMEM)] + [hbm] * 5,
            out_specs=(vmem, vmem),
            scratch_shapes=[
                pltpu.VMEM((5, rows, dt), bf), pltpu.VMEM((5, rows, ds), bf),
                pltpu.VMEM((2, rows, dt), bf), pltpu.VMEM((2, rows, ds), bf),
                pltpu.VMEM((2, 8, rows), jnp.int32),
                pltpu.VMEM((2, rows, ds), f32), pltpu.VMEM((5, rows, ds), f32),
                pltpu.VMEM((5, rows, ds), WIRE), pltpu.VMEM((5, rows, ds), WIRE),
                pltpu.VMEM((5, 8, 128), f32), pltpu.VMEM((5, 8, 128), f32),
                dma((5,)), dma((4,)), dma((4,)), dma((5,)), dma((5,)),
                dma((3,)), dma((3,)), dma((5,)), dma((5,)), dma((5,)), dma((5,)),
            ],
            compiler_params=pltpu.CompilerParams(
                collective_id=0, has_side_effects=True, vmem_limit_bytes=48 * 2**20),
            cost_estimate=pl.CostEstimate(
                flops=STEPS * 4 * rows * rows * (dt + 3 * ds) // 2, bytes_accessed=8 * rows * (dt + 3 * ds),
                transcendentals=2 * STEPS * rows * rows),
        )(scalars, mi, li, mt, lt, look)

    row = P(("inner", "outer"), None)
    return jax.shard_map(
        shards, mesh=mesh,
        in_specs=(row, row, row, row, P(("inner", "outer")), P(), P()),
        out_specs=(row, row), check_vma=False)
```

```python
import jax
import jax.numpy as jnp
from jax import lax
from jax.experimental import pallas as pl
from jax.experimental.pallas import tpu as pltpu
from jax.sharding import PartitionSpec as P

STEPS = 5
WIRE = jnp.int16
TOP = 32000.0
PIECES = 2
LATE = 1
MESH = pl.DeviceIdType.MESH


def kernel(n_inner, n_outer, scalars, mi, li, mt, lt, look, img_out, txt_out,
           tm, tl, im, il, lk, acc_img, acc_txt, gsend, grecv, msend, mrecv,
           lsem, tm_s, tl_s, tm_r, tl_r, i_s, i_r, g_s, g_r, m_s, m_r):
    i, o = lax.axis_index("inner"), lax.axis_index("outer")
    c = lax.rem(o, 2)
    at = lambda d: lax.rem(i + d + n_inner, n_inner)
    up, down = lax.rem(o + 1, n_outer), lax.rem(o + n_outer - 1, n_outer)
    rows = tm.shape[1]

    def copy(src, dst, ss, rs, dev):
        return pltpu.make_async_remote_copy(
            src_ref=src, dst_ref=dst, send_sem=ss, recv_sem=rs, device_id=dev, device_id_type=MESH)

    def signal(dev):
        pl.semaphore_signal(barrier, inc=1, device_id=dev, device_id_type=MESH)

    local = [
        pltpu.make_async_copy(mi, im.at[0], lsem.at[0]),
        pltpu.make_async_copy(li, il.at[0], lsem.at[1]),
        pltpu.make_async_copy(mt, tm.at[0], lsem.at[2]),
        pltpu.make_async_copy(lt, tl.at[0], lsem.at[3]),
        pltpu.make_async_copy(look, lk.at[0], lsem.at[4]),
    ]
    def text(k, to, sem, dev):
        n = rows // PIECES
        return [copy(buf.at[k, pl.ds(q * n, n)], buf.at[to, pl.ds(q * n, n)], ss.at[sem, q], rs.at[to, q], dev)
                for buf, ss, rs in ((tm, tm_s, tm_r), (tl, tl_s, tl_r)) for q in range(PIECES)]

    def text_next(k, dev):
        return text(k, k + 1, k, dev)

    def text_last(k, dev):
        return text(k, 4, 3, dev)

    def image_back():
        dev = (at(-2), o)
        return (copy(im.at[0], im.at[1], i_s.at[0], i_r.at[0], dev),
                copy(il.at[0], il.at[1], i_s.at[1], i_r.at[1], dev),
                copy(lk.at[0], lk.at[1], i_s.at[2], i_r.at[2], dev))

    def grad(k, slot, dev):
        return (copy(msend.at[k], mrecv.at[slot], m_s.at[k], m_r.at[slot], dev),
                copy(gsend.at[k], grecv.at[slot], g_s.at[k], g_r.at[slot], dev))

    def send_grad(k, slot, dev, x):
        top = jnp.maximum(jnp.max(jnp.abs(x)), 1e-30)
        msend[k] = jnp.full(msend.shape[1:], top, jnp.float32)
        gsend[k] = jnp.round(x * (TOP / top)).astype(jnp.int32).astype(WIRE)
        for cp in grad(k, slot, dev):
            cp.start()

    def received(slot):
        for cp in grad(0, slot, (i, o)):
            cp.wait_recv()
        return grecv[slot].astype(jnp.int32).astype(jnp.float32) * (mrecv[slot, 0:1, 0:1] * (1.0 / TOP))

    for cp in local:
        cp.start()
    barrier = pltpu.get_barrier_semaphore()
    signal((at(-1), o))

    @pl.when(c == 0)
    def _():
        signal((at(-3), down))
        pl.semaphore_wait(barrier, 2)

    @pl.when(c == 1)
    def _():
        signal((at(2), o))
        signal((at(1), o))
        signal((at(-2), o))
        signal((i, down))
        pl.semaphore_wait(barrier, 5)

    for cp in local:
        cp.wait()
    for cp in text_next(0, (at(1), o)):
        cp.start()

    @pl.when(c == 1)
    def _():
        for cp in image_back():
            cp.start()
        if LATE == 0:
            for cp in text_last(0, (at(3), up)):
                cp.start()

    acc_img[...] = jnp.zeros_like(acc_img)
    acc_txt[...] = jnp.zeros_like(acc_txt)
    sharp, offset = scalars[0], scalars[1]

    def step(s, carry):
        u = lax.rem(s // 2, 2)
        a, b = c * u, s - 2 * c * u

        @pl.when((c == 0) & (s > 0) & (s < 3))
        def _():
            for w, cp in zip(text_next(s - 1, (i, o)), text_next(s, (at(1), o))):
                w.wait_recv()
                cp.start()

        @pl.when((c == 0) & (s == 3))
        def _():
            for w, cp in zip(text_next(2, (i, o)), text_last(3, (i, up))):
                w.wait_recv()
                cp.start()

        @pl.when((c == 1) & (s == 1))
        def _():
            for w in text_next(0, (i, o)):
                w.wait_recv()

        if LATE == 1:
            @pl.when((c == 1) & (s == 1))
            def _():
                for cp in text_last(0, (at(3), up)):
                    cp.start()

        @pl.when((c == 1) & (s == 2))
        def _():
            for w in image_back():
                w.wait_recv()
            if LATE == 2:
                for cp in text_last(0, (at(3), up)):
                    cp.start()

        @pl.when(s == 4)
        def _():
            for w in text_last(0, (i, o)):
                w.wait_recv()

        dims = (((1,), (1,)), ((), ()))
        teacher = lax.dot_general(im[a], tm[b], dims, preferred_element_type=jnp.float32)
        prob = jax.nn.sigmoid(4.0 * teacher - 2.0)
        student = sharp * lax.dot_general(
            il[a], tl[b], dims, preferred_element_type=jnp.float32) + offset
        r = lax.broadcasted_iota(jnp.int32, (rows, rows), 0)
        q = lax.broadcasted_iota(jnp.int32, (rows, rows), 1)
        hit = (r == q) & (lk[a, 0:1, :] == s)
        target = 0.5 * (jnp.where(hit, 1.0, 0.0) + prob)
        g = (jax.nn.sigmoid(student) - target).astype(jnp.bfloat16)
        acc_img[a] += jnp.dot(g, tl[b], preferred_element_type=jnp.float32)
        acc_txt[b] += lax.dot_general(
            g, il[a], (((0,), (0,)), ((), ())), preferred_element_type=jnp.float32)

        @pl.when((c == 0) & (s == 0))
        def _():
            send_grad(0, 1, (at(1), o), acc_txt[0])

        @pl.when((c == 0) & (s > 0) & (s < 3))
        def _():
            send_grad(s, s + 1, (at(1), o), acc_txt[s] + received(s))

        @pl.when((c == 0) & (s == 3))
        def _():
            send_grad(3, 4, (i, up), acc_txt[3] + received(3))

        @pl.when((c == 1) & (s == 3))
        def _():
            send_grad(1, 1, (at(-1), o), acc_txt[1])
            send_grad(4, 0, (at(2), o), acc_img[1])
            send_grad(0, 4, (at(3), up), acc_txt[0] + received(1))

        return carry

    lax.fori_loop(0, STEPS, step, 0)
    scale = sharp / STEPS

    @pl.when(c == 0)
    def _():
        img_out[...] = scale * acc_img[0]

    @pl.when(c == 1)
    def _():
        img_out[...] = scale * (acc_img[0] + received(0))

    txt_out[...] = scale * (acc_txt[4] + received(4))

    def sent(copies):
        for cp in copies:
            cp.wait_send()

    sent(text_next(0, (i, o)) + text_last(0, (i, o)))
    sent(grad(0, 4, (i, o)) + grad(1, 4, (i, o)))

    @pl.when(c == 0)
    def _():
        sent(text_next(1, (i, o)) + text_next(2, (i, o)))
        sent(grad(2, 4, (i, o)) + grad(3, 4, (i, o)))

    @pl.when(c == 1)
    def _():
        sent(image_back() + grad(4, 0, (i, o)))


def solution(mesh):
    n_inner, n_outer = mesh.shape["inner"], mesh.shape["outer"]

    def shards(mi, li, mt, lt, lookup, sharpness, offset):
        rows, dt = mi.shape
        ds = li.shape[1]
        scalars = jnp.stack([sharpness, offset])
        look = jnp.broadcast_to(lookup[None, :], (8, rows))
        hbm = pl.BlockSpec(memory_space=pl.ANY)
        vmem = pl.BlockSpec(memory_space=pltpu.VMEM)
        bf, f32, dma = jnp.bfloat16, jnp.float32, pltpu.SemaphoreType.DMA
        return pl.pallas_call(
            lambda *refs: kernel(n_inner, n_outer, *refs),
            out_shape=(jax.ShapeDtypeStruct((rows, ds), f32), jax.ShapeDtypeStruct((rows, ds), f32)),
            in_specs=[pl.BlockSpec(memory_space=pltpu.SMEM)] + [hbm] * 5,
            out_specs=(vmem, vmem),
            scratch_shapes=[
                pltpu.VMEM((5, rows, dt), bf), pltpu.VMEM((5, rows, ds), bf),
                pltpu.VMEM((2, rows, dt), bf), pltpu.VMEM((2, rows, ds), bf),
                pltpu.VMEM((2, 8, rows), jnp.int32),
                pltpu.VMEM((2, rows, ds), f32), pltpu.VMEM((5, rows, ds), f32),
                pltpu.VMEM((5, rows, ds), WIRE), pltpu.VMEM((5, rows, ds), WIRE),
                pltpu.VMEM((5, 8, 128), f32), pltpu.VMEM((5, 8, 128), f32),
                dma((5,)), dma((4, PIECES)), dma((4, PIECES)), dma((5, PIECES)), dma((5, PIECES)),
                dma((3,)), dma((3,)), dma((5,)), dma((5,)), dma((5,)), dma((5,)),
            ],
            compiler_params=pltpu.CompilerParams(
                collective_id=0, has_side_effects=True, vmem_limit_bytes=60 * 2**20),
            cost_estimate=pl.CostEstimate(
                flops=STEPS * 4 * rows * rows * (dt + 3 * ds) // 2, bytes_accessed=8 * rows * (dt + 3 * ds),
                transcendentals=2 * STEPS * rows * rows),
        )(scalars, mi, li, mt, lt, look)

    row = P(("inner", "outer"), None)
    return jax.shard_map(
        shards, mesh=mesh,
        in_specs=(row, row, row, row, P(("inner", "outer")), P(), P()),
        out_specs=(row, row), check_vma=False)
```

```python
import jax
import jax.numpy as jnp
from jax import lax
from jax.experimental import pallas as pl
from jax.experimental.pallas import tpu as pltpu
from jax.sharding import PartitionSpec as P

STEPS = 5
WIRE = jnp.int16
TOP = 32000.0
PIECES = 2
LATE = 1
MESH = pl.DeviceIdType.MESH


def kernel(n_inner, n_outer, scalars, mi, li, mt, lt, look, img_out, txt_out,
           tm, tl, im, il, lk, acc_img, acc_txt, gsend, grecv, msend, mrecv,
           lsem, tm_s, tl_s, tm_r, tl_r, i_s, i_r, g_s, g_r, m_s, m_r):
    i, o = lax.axis_index("inner"), lax.axis_index("outer")
    c = lax.rem(o, 2)
    at = lambda d: lax.rem(i + d + n_inner, n_inner)
    up, down = lax.rem(o + 1, n_outer), lax.rem(o + n_outer - 1, n_outer)
    z = lax.rem(i, 6)
    rows = tm.shape[1]

    def copy(src, dst, ss, rs, dev):
        return pltpu.make_async_remote_copy(
            src_ref=src, dst_ref=dst, send_sem=ss, recv_sem=rs, device_id=dev, device_id_type=MESH)

    def signal(dev):
        pl.semaphore_signal(barrier, inc=1, device_id=dev, device_id_type=MESH)

    local = [
        pltpu.make_async_copy(mi, im.at[0], lsem.at[0]),
        pltpu.make_async_copy(li, il.at[0], lsem.at[1]),
        pltpu.make_async_copy(mt, tm.at[0], lsem.at[2]),
        pltpu.make_async_copy(lt, tl.at[0], lsem.at[3]),
        pltpu.make_async_copy(look, lk.at[0], lsem.at[4]),
    ]
    def text(k, to, sem, dev):
        n = rows // PIECES
        return [copy(buf.at[k, pl.ds(q * n, n)], buf.at[to, pl.ds(q * n, n)], ss.at[sem, q], rs.at[to, q], dev)
                for buf, ss, rs in ((tm, tm_s, tm_r), (tl, tl_s, tl_r)) for q in range(PIECES)]

    def text_next(k, dev):
        return text(k, k + 1, k, dev)

    def text_over(d):
        return text(0, d, 4, (at(d), o))

    def text_last(k, dev):
        return text(k, 4, 3, dev)

    def image_back():
        dev = (at(-2), o)
        return (copy(im.at[0], im.at[1], i_s.at[0], i_r.at[0], dev),
                copy(il.at[0], il.at[1], i_s.at[1], i_r.at[1], dev),
                copy(lk.at[0], lk.at[1], i_s.at[2], i_r.at[2], dev))

    def grad(k, slot, dev):
        return (copy(msend.at[k], mrecv.at[slot], m_s.at[k], m_r.at[slot], dev),
                copy(gsend.at[k], grecv.at[slot], g_s.at[k], g_r.at[slot], dev))

    def send_grad(k, slot, dev, x):
        top = jnp.maximum(jnp.max(jnp.abs(x)), 1e-30)
        msend[k] = jnp.full(msend.shape[1:], top, jnp.float32)
        gsend[k] = jnp.round(x * (TOP / top)).astype(jnp.int32).astype(WIRE)
        for cp in grad(k, slot, dev):
            cp.start()

    def received(slot):
        for cp in grad(0, slot, (i, o)):
            cp.wait_recv()
        return grecv[slot].astype(jnp.int32).astype(jnp.float32) * (mrecv[slot, 0:1, 0:1] * (1.0 / TOP))

    for cp in local:
        cp.start()
    barrier = pltpu.get_barrier_semaphore()
    signal((at(-1), o))

    @pl.when(c == 0)
    def _():
        signal((at(-3), down))

        @pl.when(z == 0)
        def _():
            signal((at(-3), o))

        pl.semaphore_wait(barrier, 2 + z // 3 - z // 4)

    @pl.when(c == 1)
    def _():
        signal((at(2), o))
        signal((at(1), o))
        signal((at(-2), o))
        signal((i, down))
        pl.semaphore_wait(barrier, 5)

    for cp in local:
        cp.wait()
    for cp in text_next(0, (at(1), o)):
        cp.start()

    @pl.when(c == 1)
    def _():
        for cp in image_back():
            cp.start()
        if LATE == 0:
            for cp in text_last(0, (at(3), up)):
                cp.start()

    acc_img[...] = jnp.zeros_like(acc_img)
    acc_txt[...] = jnp.zeros_like(acc_txt)
    sharp, offset = scalars[0], scalars[1]

    def step(s, carry):
        u = lax.rem(s // 2, 2)
        a, b = c * u, s - c * u * (2 * s - 3)
        label = s - c * u * (2 * s - 5)

        @pl.when((c == 0) & (s > 0) & (s < 3))
        def _():
            for w, cp in zip(text_next(s - 1, (i, o)), text_next(s, (at(1), o))):
                w.wait_recv()

                @pl.when((z <= 4) | (s == 1))
                def _():
                    cp.start()

        @pl.when((c == 0) & (s == 3))
        def _():
            for w, cp in zip(text_next(2, (i, o)), text_last(3, (i, up))):
                w.wait_recv()
                cp.start()

        @pl.when((c == 1) & (s == 1))
        def _():
            for w in text_next(0, (i, o)):
                w.wait_recv()

        @pl.when((c == 0) & (s == 3) & (z == 3))
        def _():
            for cp in text_over(3):
                cp.start()

        if LATE == 1:
            @pl.when((c == 1) & (s == 1))
            def _():
                for cp in text_last(0, (at(3), up)):
                    cp.start()

        @pl.when((c == 1) & (s == 2))
        def _():
            for w in image_back():
                w.wait_recv()
            if LATE == 2:
                for cp in text_last(0, (at(3), up)):
                    cp.start()

        @pl.when(s == 4)
        def _():
            for w in text_last(0, (i, o)):
                w.wait_recv()

        dims = (((1,), (1,)), ((), ()))
        teacher = lax.dot_general(im[a], tm[b], dims, preferred_element_type=jnp.float32)
        prob = jax.nn.sigmoid(4.0 * teacher - 2.0)
        student = sharp * lax.dot_general(
            il[a], tl[b], dims, preferred_element_type=jnp.float32) + offset
        r = lax.broadcasted_iota(jnp.int32, (rows, rows), 0)
        q = lax.broadcasted_iota(jnp.int32, (rows, rows), 1)
        hit = (r == q) & (lk[a, 0:1, :] == label)
        target = 0.5 * (jnp.where(hit, 1.0, 0.0) + prob)
        g = (jax.nn.sigmoid(student) - target).astype(jnp.bfloat16)
        acc_img[a] += jnp.dot(g, tl[b], preferred_element_type=jnp.float32)
        acc_txt[b] += lax.dot_general(
            g, il[a], (((0,), (0,)), ((), ())), preferred_element_type=jnp.float32)

        @pl.when((c == 0) & (s == 0))
        def _():
            send_grad(0, 1, (at(1), o), acc_txt[0])

        @pl.when((c == 0) & (s > 0) & (s < 3))
        def _():
            send_grad(s, s + 1, (at(1), o), acc_txt[s] + received(s))

        @pl.when((c == 0) & (s == 3))
        def _():
            send_grad(3, 4, (i, up), acc_txt[3] + received(3))

        @pl.when((c == 1) & (s == 2))
        def _():
            send_grad(1, 1, (at(-1), o), acc_txt[1])

        @pl.when((c == 1) & (s == 3))
        def _():
            send_grad(4, 0, (at(2), o), acc_img[1])
            send_grad(0, 4, (at(3), up), acc_txt[0] + received(1))

        return carry

    lax.fori_loop(0, STEPS, step, 0)
    scale = sharp / STEPS

    @pl.when(c == 0)
    def _():
        img_out[...] = scale * acc_img[0]

    @pl.when(c == 1)
    def _():
        img_out[...] = scale * (acc_img[0] + received(0))

    txt_out[...] = scale * (acc_txt[4] + received(4))

    def sent(copies):
        for cp in copies:
            cp.wait_send()

    sent(text_next(0, (i, o)) + text_last(0, (i, o)))
    sent(grad(0, 4, (i, o)) + grad(1, 4, (i, o)))

    @pl.when(c == 0)
    def _():
        sent(text_next(1, (i, o)))

        @pl.when(z <= 4)
        def _():
            sent(text_next(2, (i, o)))

        @pl.when(z == 3)
        def _():
            sent(text_over(2))

        sent(grad(2, 4, (i, o)) + grad(3, 4, (i, o)))

    @pl.when(c == 1)
    def _():
        sent(image_back() + grad(4, 0, (i, o)))


def solution(mesh):
    n_inner, n_outer = mesh.shape["inner"], mesh.shape["outer"]

    def shards(mi, li, mt, lt, lookup, sharpness, offset):
        rows, dt = mi.shape
        ds = li.shape[1]
        scalars = jnp.stack([sharpness, offset])
        look = jnp.broadcast_to(lookup[None, :], (8, rows))
        hbm = pl.BlockSpec(memory_space=pl.ANY)
        vmem = pl.BlockSpec(memory_space=pltpu.VMEM)
        bf, f32, dma = jnp.bfloat16, jnp.float32, pltpu.SemaphoreType.DMA
        return pl.pallas_call(
            lambda *refs: kernel(n_inner, n_outer, *refs),
            out_shape=(jax.ShapeDtypeStruct((rows, ds), f32), jax.ShapeDtypeStruct((rows, ds), f32)),
            in_specs=[pl.BlockSpec(memory_space=pltpu.SMEM)] + [hbm] * 5,
            out_specs=(vmem, vmem),
            scratch_shapes=[
                pltpu.VMEM((5, rows, dt), bf), pltpu.VMEM((5, rows, ds), bf),
                pltpu.VMEM((2, rows, dt), bf), pltpu.VMEM((2, rows, ds), bf),
                pltpu.VMEM((2, 8, rows), jnp.int32),
                pltpu.VMEM((2, rows, ds), f32), pltpu.VMEM((5, rows, ds), f32),
                pltpu.VMEM((5, rows, ds), WIRE), pltpu.VMEM((5, rows, ds), WIRE),
                pltpu.VMEM((5, 8, 128), f32), pltpu.VMEM((5, 8, 128), f32),
                dma((5,)), dma((5, PIECES)), dma((5, PIECES)), dma((5, PIECES)), dma((5, PIECES)),
                dma((3,)), dma((3,)), dma((5,)), dma((5,)), dma((5,)), dma((5,)),
            ],
            compiler_params=pltpu.CompilerParams(
                collective_id=0, has_side_effects=True, vmem_limit_bytes=60 * 2**20),
            cost_estimate=pl.CostEstimate(
                flops=STEPS * 4 * rows * rows * (dt + 3 * ds) // 2, bytes_accessed=8 * rows * (dt + 3 * ds),
                transcendentals=2 * STEPS * rows * rows),
        )(scalars, mi, li, mt, lt, look)

    row = P(("inner", "outer"), None)
    return jax.shard_map(
        shards, mesh=mesh,
        in_specs=(row, row, row, row, P(("inner", "outer")), P(), P()),
        out_specs=(row, row), check_vma=False)
```

```python
import jax
import jax.numpy as jnp
from jax import lax
from jax.experimental import pallas as pl
from jax.experimental.pallas import tpu as pltpu
from jax.sharding import PartitionSpec as P

STEPS = 5
WIRE = jnp.int16
TOP = 32000.0
PIECES = 2
LATE = 1
MESH = pl.DeviceIdType.MESH


def kernel(n_inner, n_outer, scalars, mi, li, mt, lt, look, img_out, txt_out,
           tm, tl, im, il, lk, acc_img, acc_txt, gsend, grecv, msend, mrecv,
           lsem, tm_s, tl_s, tm_r, tl_r, i_s, i_r, g_s, g_r, m_s, m_r):
    i, o = lax.axis_index("inner"), lax.axis_index("outer")
    c = lax.rem(o, 2)
    at = lambda d: lax.rem(i + d + n_inner, n_inner)
    up, down = lax.rem(o + 1, n_outer), lax.rem(o + n_outer - 1, n_outer)
    z = lax.rem(i, 6)
    rows = tm.shape[1]

    def copy(src, dst, ss, rs, dev):
        return pltpu.make_async_remote_copy(
            src_ref=src, dst_ref=dst, send_sem=ss, recv_sem=rs, device_id=dev, device_id_type=MESH)

    def signal(dev):
        pl.semaphore_signal(barrier, inc=1, device_id=dev, device_id_type=MESH)

    local = [
        pltpu.make_async_copy(mi, im.at[0], lsem.at[0]),
        pltpu.make_async_copy(li, il.at[0], lsem.at[1]),
        pltpu.make_async_copy(mt, tm.at[0], lsem.at[2]),
        pltpu.make_async_copy(lt, tl.at[0], lsem.at[3]),
        pltpu.make_async_copy(look, lk.at[0], lsem.at[4]),
    ]
    def text(k, to, sem, dev):
        n = rows // PIECES
        return [copy((own if isinstance(k, int) and k == 0 else buf.at[k]).at[pl.ds(q * n, n)], buf.at[to, pl.ds(q * n, n)], ss.at[sem, q], rs.at[to, q], dev)
                for buf, own, ss, rs in ((tm, mt, tm_s, tm_r), (tl, lt, tl_s, tl_r)) for q in range(PIECES)]

    def text_next(k, dev):
        return text(k, k + 1, k, dev)

    def text_over(d):
        return text(0, d, 4, (at(d), o))

    def text_last(k, dev):
        return text(k, 4, 3, dev)

    def image_back():
        dev = (at(-2), o)
        return (copy(mi, im.at[1], i_s.at[0], i_r.at[0], dev),
                copy(li, il.at[1], i_s.at[1], i_r.at[1], dev),
                copy(look, lk.at[1], i_s.at[2], i_r.at[2], dev))

    def grad(k, slot, dev):
        return (copy(msend.at[k], mrecv.at[slot], m_s.at[k], m_r.at[slot], dev),
                copy(gsend.at[k], grecv.at[slot], g_s.at[k], g_r.at[slot], dev))

    def send_grad(k, slot, dev, x):
        top = jnp.maximum(jnp.max(jnp.abs(x)), 1e-30)
        msend[k] = jnp.full(msend.shape[1:], top, jnp.float32)
        gsend[k] = jnp.round(x * (TOP / top)).astype(jnp.int32).astype(WIRE)
        for cp in grad(k, slot, dev):
            cp.start()

    def received(slot):
        for cp in grad(0, slot, (i, o)):
            cp.wait_recv()
        return grecv[slot].astype(jnp.int32).astype(jnp.float32) * (mrecv[slot, 0:1, 0:1] * (1.0 / TOP))

    for cp in local:
        cp.start()
    barrier = pltpu.get_barrier_semaphore()
    signal((at(-1), o))

    @pl.when(c == 0)
    def _():
        signal((at(-3), down))

        @pl.when(z == 0)
        def _():
            signal((at(-3), o))

        pl.semaphore_wait(barrier, 2 + z // 3 - z // 4)

    @pl.when(c == 1)
    def _():
        signal((at(2), o))
        signal((at(1), o))
        signal((at(-2), o))
        signal((i, down))
        pl.semaphore_wait(barrier, 5)

    for cp in text_next(0, (at(1), o)):
        cp.start()

    @pl.when(c == 1)
    def _():
        for cp in image_back():
            cp.start()
        if LATE == 0:
            for cp in text_last(0, (at(3), up)):
                cp.start()

    acc_img[...] = jnp.zeros_like(acc_img)
    acc_txt[...] = jnp.zeros_like(acc_txt)
    sharp, offset = scalars[0], scalars[1]
    for cp in local:
        cp.wait()

    def step(s, carry):
        u = lax.rem(s // 2, 2)
        a, b = c * u, s - c * u * (2 * s - 3)
        label = s - c * u * (2 * s - 5)

        @pl.when((c == 0) & (s > 0) & (s < 3))
        def _():
            for w, cp in zip(text_next(s - 1, (i, o)), text_next(s, (at(1), o))):
                w.wait_recv()

                @pl.when((z <= 4) | (s == 1))
                def _():
                    cp.start()

        @pl.when((c == 0) & (s == 3))
        def _():
            for w, cp in zip(text_next(2, (i, o)), text_last(3, (i, up))):
                w.wait_recv()
                cp.start()

        @pl.when((c == 1) & (s == 1))
        def _():
            for w in text_next(0, (i, o)):
                w.wait_recv()

        @pl.when((c == 0) & (s == 3) & (z == 3))
        def _():
            for cp in text_over(3):
                cp.start()

        if LATE == 1:
            @pl.when((c == 1) & (s == 1))
            def _():
                for cp in text_last(0, (at(3), up)):
                    cp.start()

        @pl.when((c == 1) & (s == 2))
        def _():
            for w in image_back():
                w.wait_recv()
            if LATE == 2:
                for cp in text_last(0, (at(3), up)):
                    cp.start()

        @pl.when(s == 4)
        def _():
            for w in text_last(0, (i, o)):
                w.wait_recv()

        dims = (((1,), (1,)), ((), ()))
        teacher = lax.dot_general(im[a], tm[b], dims, preferred_element_type=jnp.float32)
        prob = jax.nn.sigmoid(4.0 * teacher - 2.0)
        student = sharp * lax.dot_general(
            il[a], tl[b], dims, preferred_element_type=jnp.float32) + offset
        r = lax.broadcasted_iota(jnp.int32, (rows, rows), 0)
        q = lax.broadcasted_iota(jnp.int32, (rows, rows), 1)
        hit = (r == q) & (lk[a, 0:1, :] == label)
        target = 0.5 * (jnp.where(hit, 1.0, 0.0) + prob)
        g = (jax.nn.sigmoid(student) - target).astype(jnp.bfloat16)
        acc_img[a] += jnp.dot(g, tl[b], preferred_element_type=jnp.float32)
        acc_txt[b] += lax.dot_general(
            g, il[a], (((0,), (0,)), ((), ())), preferred_element_type=jnp.float32)

        @pl.when((c == 0) & (s == 0))
        def _():
            send_grad(0, 1, (at(1), o), acc_txt[0])

        @pl.when((c == 0) & (s > 0) & (s < 3))
        def _():
            send_grad(s, s + 1, (at(1), o), acc_txt[s] + received(s))

        @pl.when((c == 0) & (s == 3))
        def _():
            send_grad(3, 4, (i, up), acc_txt[3] + received(3))

        @pl.when((c == 1) & (s == 2))
        def _():
            send_grad(1, 1, (at(-1), o), acc_txt[1])

        @pl.when((c == 1) & (s == 3))
        def _():
            send_grad(4, 0, (at(2), o), acc_img[1])
            send_grad(0, 4, (at(3), up), acc_txt[0] + received(1))

        return carry

    lax.fori_loop(0, STEPS, step, 0)
    scale = sharp / STEPS

    @pl.when(c == 0)
    def _():
        img_out[...] = scale * acc_img[0]

    @pl.when(c == 1)
    def _():
        img_out[...] = scale * (acc_img[0] + received(0))

    txt_out[...] = scale * (acc_txt[4] + received(4))

    def sent(copies):
        for cp in copies:
            cp.wait_send()

    sent(text_next(0, (i, o)) + text_last(0, (i, o)))
    sent(grad(0, 4, (i, o)) + grad(1, 4, (i, o)))

    @pl.when(c == 0)
    def _():
        sent(text_next(1, (i, o)))

        @pl.when(z <= 4)
        def _():
            sent(text_next(2, (i, o)))

        @pl.when(z == 3)
        def _():
            sent(text_over(2))

        sent(grad(2, 4, (i, o)) + grad(3, 4, (i, o)))

    @pl.when(c == 1)
    def _():
        sent(image_back() + grad(4, 0, (i, o)))


def solution(mesh):
    n_inner, n_outer = mesh.shape["inner"], mesh.shape["outer"]

    def shards(mi, li, mt, lt, lookup, sharpness, offset):
        rows, dt = mi.shape
        ds = li.shape[1]
        scalars = jnp.stack([sharpness, offset])
        look = jnp.broadcast_to(lookup[None, :], (8, rows))
        hbm = pl.BlockSpec(memory_space=pl.ANY)
        vmem = pl.BlockSpec(memory_space=pltpu.VMEM)
        bf, f32, dma = jnp.bfloat16, jnp.float32, pltpu.SemaphoreType.DMA
        return pl.pallas_call(
            lambda *refs: kernel(n_inner, n_outer, *refs),
            out_shape=(jax.ShapeDtypeStruct((rows, ds), f32), jax.ShapeDtypeStruct((rows, ds), f32)),
            in_specs=[pl.BlockSpec(memory_space=pltpu.SMEM)] + [hbm] * 5,
            out_specs=(vmem, vmem),
            scratch_shapes=[
                pltpu.VMEM((5, rows, dt), bf), pltpu.VMEM((5, rows, ds), bf),
                pltpu.VMEM((2, rows, dt), bf), pltpu.VMEM((2, rows, ds), bf),
                pltpu.VMEM((2, 8, rows), jnp.int32),
                pltpu.VMEM((2, rows, ds), f32), pltpu.VMEM((5, rows, ds), f32),
                pltpu.VMEM((5, rows, ds), WIRE), pltpu.VMEM((5, rows, ds), WIRE),
                pltpu.VMEM((5, 8, 128), f32), pltpu.VMEM((5, 8, 128), f32),
                dma((5,)), dma((5, PIECES)), dma((5, PIECES)), dma((5, PIECES)), dma((5, PIECES)),
                dma((3,)), dma((3,)), dma((5,)), dma((5,)), dma((5,)), dma((5,)),
            ],
            compiler_params=pltpu.CompilerParams(
                collective_id=0, has_side_effects=True, vmem_limit_bytes=60 * 2**20),
            cost_estimate=pl.CostEstimate(
                flops=STEPS * 4 * rows * rows * (dt + 3 * ds) // 2, bytes_accessed=8 * rows * (dt + 3 * ds),
                transcendentals=2 * STEPS * rows * rows),
        )(scalars, mi, li, mt, lt, look)

    row = P(("inner", "outer"), None)
    return jax.shard_map(
        shards, mesh=mesh,
        in_specs=(row, row, row, row, P(("inner", "outer")), P(), P()),
        out_specs=(row, row), check_vma=False)
```
